128 devices in a mesh: frame: 8 (over x, core), cell: 16 (over y, z).
Axes of the slice: x: 4, y: 4, z: 4, core: 2. Of those that a mesh axis runs over, the one named last changes fastest.
Arguments:
- front: float32 [8, 4096, 4096], P('frame', 'cell')
- parent_of: int32 [8], replicated, may hold values from 0 to 7
- block_map: int32 [8, 13], replicated, may hold values from 3 to 31, as said below
- parent_in: bfloat16 [8, 2, 4096, 8192], P('frame', None, 'cell'), may hold values from -0.3125 to 0.3125
Outputs:
- lower_panel: float32 [8, 4096, 768], P('frame', 'cell')
- parent_out: bfloat16 [8, 2, 4096, 8192], P('frame', None, 'cell')
The draws below stay inside these ranges and needn't reach their ends.
Inputs may be any that keep to these rules, and one draw needn't show every extreme that they name: block_map[c, k] is 3 + k or 3 + k + 16.
All inputs are finite; a program needn't handle non-finite values.
Results may differ from the reference program's by a relative error of at most 0.004.
Values may be sent and summed in bfloat16 or wider, within the bound.
A program may use at most 192 MiB of HBM per device.

```python
import math
import jax
import jax.numpy as jnp
import numpy as np
from jax import lax

BLK = 256
PB = 3
NB = 16
UB = 13
NBP = 32
FRONTS = 8
PARENTS = 8


def draw_front(key, part):
    keys = jax.random.split(key, 4)
    width = PB * BLK
    order = NB * BLK
    rest = order - width
    highest = lax.Precision.HIGHEST
    mixing = jax.random.normal(keys[0], (FRONTS, width, width), jnp.float32)
    leading = jnp.einsum('fik,fjk->fij', mixing, mixing, precision=highest) / width
    leading = 0.5 * (leading + jnp.transpose(leading, (0, 2, 1)))
    small_rows = jnp.arange(width)
    small_ident = (small_rows[:, None] == small_rows[None, :]).astype(jnp.float32)
    leading = leading + small_ident[None, :, :]
    coupling = jax.random.normal(keys[1], (FRONTS, width, rest), jnp.float32) / math.sqrt(width)
    gram = jnp.einsum('fki,fkj->fij', coupling, coupling, precision=highest)
    gram = 0.5 * (gram + jnp.transpose(gram, (0, 2, 1)))
    jitter = jax.random.uniform(keys[2], (FRONTS, rest, rest), jnp.float32, -1.0, 1.0)
    jitter = (jitter + jnp.transpose(jitter, (0, 2, 1))) * (0.125 / rest)
    base = jax.random.uniform(keys[3], (FRONTS, rest), jnp.float32, 0.5, 1.0)
    rest_rows = jnp.arange(rest)
    rest_ident = (rest_rows[:, None] == rest_rows[None, :]).astype(jnp.float32)
    trailing = gram + jitter + rest_ident[None, :, :] * base[:, :, None]
    upper_rows = jnp.concatenate([leading, coupling], 2)
    lower_rows = jnp.concatenate([jnp.transpose(coupling, (0, 2, 1)), trailing], 2)
    matrix = jnp.concatenate([upper_rows, lower_rows], 1)
    return matrix.astype(jnp.float32)


def draw_block_map(key, part):
    upper = jax.random.randint(key, (FRONTS, NB - PB), 0, 2)
    upper = upper.at[0, 0].set(0)
    upper = upper.at[0, NB - PB - 1].set(1)
    steps = jnp.arange(NB - PB, dtype=jnp.int32)
    return (PB + steps[None, :] + NB * upper).astype(jnp.int32)


def set_ends(values, stream_key, least, high):
    shape = values.shape
    place = [jax.random.randint(jax.random.fold_in(stream_key, axis), (), 0, shape[axis]) for axis in range(len(shape))]
    values = values.at[tuple(place)].set(least)
    longest = shape.index(max(shape))
    place[longest] = (place[longest] + 1) % shape[longest]
    return values.at[tuple(place)].set(high)


def block_levels(own_key, dims, pieces, low, top_value):
    def one(axis_at, parts):
        heights = jax.random.uniform(jax.random.fold_in(jax.random.fold_in(own_key, 6), axis_at), (parts,), jnp.float32, low / len(pieces), top_value / len(pieces))
        return jnp.repeat(jnp.exp(heights), dims[axis_at] // parts).reshape((-1,) + (1,) * (len(dims) - axis_at - 1))

    loudness = one(*pieces[0])
    for cut in pieces[1:]:
        loudness = loudness * one(*cut)
    return loudness


def cumulative_ranks(amount, skew):
    weights = [(1 << 20) // math.isqrt(grade ** skew) + 1 for grade in range(1, amount + 1)]
    scale = 1 + sum(weights) // (1 << 30)
    return np.cumsum(np.array([max(1, weight // scale) for weight in weights]))


def ranked(rng, extent, number_of, skew):
    listing = cumulative_ranks(number_of, skew)
    pick = jax.random.randint(jax.random.fold_in(rng, 1), extent, 0, int(listing[number_of - 1]))
    standing = jnp.searchsorted(jnp.asarray(listing, jnp.int32), pick, side="right")
    return jax.random.permutation(jax.random.fold_in(rng, 2), number_of)[standing].astype(jnp.int32)


def bell_draw(stream_key, dims, scale, reach, pieces=(), kind=jnp.bfloat16):
    result = jax.random.normal(stream_key, dims, jnp.float32) * scale
    if len(pieces) > 0:
        result = block_levels(stream_key, dims, pieces, -0.22, 0.18) * result
    return jnp.clip(result, min=-reach, max=reach).astype(kind)


def setup_inputs(seed: int = 0) -> dict:
    key_of = jax.random.split(jax.random.key(seed), 5)
    front = draw_front(jax.random.fold_in(key_of[4], 71), 0)
    parent_of = set_ends(ranked(key_of[1], (FRONTS,), PARENTS, 2), jax.random.fold_in(key_of[1], 3), 0, PARENTS - 1).astype(jnp.int32)
    block_map = draw_block_map(jax.random.fold_in(key_of[4], 71), 0)
    parent_in = bell_draw(key_of[3], (PARENTS, 2, NB * BLK, NBP * BLK), 0.02, 0.3125, ((0, 8), (2, 16)))
    return dict(front=front, parent_of=parent_of, block_map=block_map, parent_in=parent_in)


def factor_one(matrix):
    width = PB * BLK
    l11 = jnp.linalg.cholesky(matrix[:width, :width])
    l21 = lax.linalg.triangular_solve(l11, matrix[width:, :width], left_side=False, lower=True, transpose_a=True)
    update = matrix[width:, width:] - jnp.dot(l21, l21.T, precision=lax.Precision.HIGHEST)
    return (jnp.concatenate([l11, l21], 0), update.astype(jnp.bfloat16))

def spread_one(update, positions):
    onehot = (positions[:, None] == jnp.arange(NBP, dtype=jnp.int32)[None, :]).astype(jnp.float32)
    blocks = update.astype(jnp.float32).reshape(UB, BLK, UB, BLK)
    placed = jnp.einsum('kalb,kj,lm->jamb', blocks, onehot, onehot)
    return placed.reshape(NBP * BLK, NBP * BLK)

def reference(front, parent_of, block_map, parent_in):
    panels = []
    totals = parent_in.astype(jnp.float32).reshape(PARENTS, NBP * BLK, NBP * BLK)
    for child in range(FRONTS):
        panel, update = factor_one(front[child])
        panels.append(panel)
        totals = totals.at[parent_of[child]].add(spread_one(update, block_map[child]))
    parent_out = totals.reshape(PARENTS, 2, NB * BLK, NBP * BLK).astype(jnp.bfloat16)
    return (jnp.stack(panels, 0), parent_out)
```

```python
import functools

import jax
import jax.numpy as jnp
from jax import lax
from jax.experimental import pallas as pl
from jax.experimental.pallas import tpu as pltpu
from jax.sharding import PartitionSpec as P

PB = 3
BLK = 256
F32, BF16 = jnp.float32, jnp.bfloat16
NT = (((1,), (1,)), ((), ()))
TN = (((0,), (0,)), ((), ()))
STRIP = 16
SIDE = 4
CELLS = SIDE * SIDE
FRAMES = 2 * SIDE
WIDTH = PB * BLK
OFFSET = (0, BLK, 3 * BLK)
PACKED = 6 * BLK
PART = BLK // CELLS
VMEM = pltpu.VMEM
DMA = pltpu.SemaphoreType.DMA
MESH = pl.DeviceIdType.MESH


def remote(src, dst, send, recv, frame, cell):
    return pltpu.make_async_remote_copy(
        src_ref=src, dst_ref=dst, send_sem=send, recv_sem=recv,
        device_id=(frame, cell), device_id_type=MESH,
    )


def greet(devices):
    barrier = pltpu.get_barrier_semaphore()
    for frame, cell in devices:
        pl.semaphore_signal(barrier, inc=1, device_id=(frame, cell), device_id_type=MESH)
    pl.semaphore_wait(barrier, len(devices))


def pivot_kernel(front, packed, part, send1, recv1, local1, send2, recv2, local2):
    frame, cell = lax.axis_index("frame"), lax.axis_index("cell")
    greet([(frame, lax.rem(cell + i, CELLS)) for i in range(1, CELLS)])

    def scatter(r, d):
        wide = BLK * (r + 1)
        src = front.at[pl.ds(pl.multiple_of(d * PART, PART), PART), pl.ds(0, wide)]
        return src, part.at[:, pl.ds(OFFSET[r], wide)]

    for r in range(PB):
        @pl.when(cell == r)
        def _(r=r):
            for i in range(1, CELLS):
                d = lax.rem(r + i, CELLS)
                src, dst = scatter(r, d)
                remote(src, dst, send1.at[i], recv1.at[r], frame, d).start()
            src, dst = scatter(r, r)
            own = pltpu.make_async_copy(src, dst, local1)
            own.start()
            own.wait()

    for r in range(PB):
        @pl.when(cell != r)
        def _(r=r):
            src, dst = scatter(r, cell)
            remote(src, dst, send1.at[0], recv1.at[r], frame, r).wait_recv()

    keep = pltpu.make_async_copy(part, packed.at[cell], local2)
    keep.start()
    for i in range(1, CELLS):
        d = lax.rem(cell + i, CELLS)
        remote(part, packed.at[cell], send2.at[i], recv2.at[cell], frame, d).start()
    for i in range(1, CELLS):
        d = lax.rem(cell + i, CELLS)
        remote(part, packed.at[d], send2.at[i], recv2.at[d], frame, d).wait()
    keep.wait()
    for r in range(PB):
        @pl.when(cell == r)
        def _(r=r):
            for i in range(1, CELLS):
                d = lax.rem(r + i, CELLS)
                src, dst = scatter(r, d)
                remote(src, dst, send1.at[i], recv1.at[r], frame, d).wait_send()


def gather_pivot(front):
    return pl.pallas_call(
        pivot_kernel,
        out_shape=jax.ShapeDtypeStruct((CELLS, PART, PACKED), F32),
        in_specs=[pl.BlockSpec(memory_space=pl.ANY)],
        out_specs=pl.BlockSpec(memory_space=pl.ANY),
        scratch_shapes=[
            VMEM((PART, PACKED), F32),
            DMA((CELLS,)), DMA((PB,)), DMA, DMA((CELLS,)), DMA((CELLS,)), DMA,
        ],
        compiler_params=pltpu.CompilerParams(collective_id=1, has_side_effects=True),
        name="gather_pivot",
    )(front)


def split(x):
    hi = x.astype(BF16)
    return hi, (x - hi.astype(F32)).astype(BF16)


def dot3(a, b, dims):
    def one(u, v):
        return lax.dot_general(u, v, dims, preferred_element_type=F32)

    return one(a[0], b[0]) + one(a[0], b[1]) + one(a[1], b[0])


def strip_step(s, work, done):
    first = pl.multiple_of(s * STRIP, STRIP)
    rows = work[pl.ds(first, STRIP), :]
    left, right = rows[:, :128], rows[:, 128:]
    turned = pltpu.roll(left, lax.rem(128 - first, 128), 1)
    cols = [jnp.broadcast_to(turned[:, b:b + 1], (STRIP, 128)) for b in range(STRIP)]
    row_no = lax.broadcasted_iota(jnp.int32, (STRIP, 128), 0)
    lane = lax.broadcasted_iota(jnp.int32, (STRIP, 128), 1)
    scale = jnp.zeros((STRIP, 128), F32)
    for a in range(STRIP):
        below = jnp.where(row_no > a, cols[a], 0.0)
        root = jnp.broadcast_to(lax.rsqrt(cols[a][a:a + 1, :]), (STRIP, 128))
        over = root * root
        scale = jnp.where(row_no == a, root, scale)
        if a < STRIP - 1:
            for b in range(a + 1, STRIP):
                cols[b] = cols[b] - (below * cols[b][a:a + 1, :]) * over
            ratio = below * over
            left = left - ratio * left[a:a + 1, :]
            right = right - ratio * right[a:a + 1, :]
    upper = jnp.where(lane >= row_no + first, left * scale, 0.0)
    inverse = right * scale
    done[pl.ds(first, STRIP), :128] = upper
    done[pl.ds(first, STRIP), 128:] = inverse
    u1, u2 = split(upper)
    v1, v2 = split(inverse)
    one, two = jnp.concatenate([u1, v1], 1), jnp.concatenate([u2, v2], 1)
    work[...] -= lax.dot_general(
        jnp.concatenate([u1, u1, u2], 0), jnp.concatenate([one, two, one], 0), TN,
        preferred_element_type=F32,
    )


def factor_kernel(where_ref, packed, own, lower, panel, a, work, done):
    for r in range(PB):
        a[BLK * r:BLK * (r + 1), :BLK * (r + 1)] = packed[:, OFFSET[r]:OFFSET[r] + BLK * (r + 1)]
    a[WIDTH:] = own[...]
    blocks = WIDTH // 128
    eye = (
        lax.broadcasted_iota(jnp.int32, (128, 128), 0)
        == lax.broadcasted_iota(jnp.int32, (128, 128), 1)
    ).astype(F32)
    for j in range(blocks):
        lo, hi = 128 * j, 128 * (j + 1)
        work[:, :128] = a[lo:hi, lo:hi]
        work[:, 128:] = eye

        def step(s, carry):
            strip_step(s, work, done)
            return carry

        lax.fori_loop(0, 128 // STRIP, step, 0)
        inverse = split(done[:, 128:])
        a[lo:hi, lo:hi] = done[:, :128].T
        below = dot3(split(a[hi:, lo:hi]), inverse, NT)
        a[hi:, lo:hi] = below
        p1, p2 = split(below)
        for k in range(j + 1, blocks):
            o = 128 * (k - j - 1)
            a[128 * k:, 128 * k:128 * (k + 1)] -= dot3(
                (p1[o:], p2[o:]), (p1[o:o + 128], p2[o:o + 128]), NT
            )
    start = pl.multiple_of(where_ref[0], BLK)
    mine = a[pl.ds(start, BLK), :]
    row_no = lax.broadcasted_iota(jnp.int32, (BLK, WIDTH), 0) + start
    col_no = lax.broadcasted_iota(jnp.int32, (BLK, WIDTH), 1)
    lower[...] = jnp.where(row_no >= col_no, mine, 0.0)
    panel[...] = a[WIDTH:].astype(BF16)


def factor(where, packed, own):
    spec = pl.BlockSpec(memory_space=VMEM)
    return pl.pallas_call(
        factor_kernel,
        out_shape=(
            jax.ShapeDtypeStruct((BLK, WIDTH), F32),
            jax.ShapeDtypeStruct((BLK, WIDTH), BF16),
        ),
        in_specs=[pl.BlockSpec(memory_space=pltpu.SMEM), spec, spec],
        out_specs=(spec, spec),
        scratch_shapes=[
            VMEM((WIDTH + BLK, WIDTH), F32), VMEM((128, 256), F32), VMEM((128, 256), F32),
        ],
        compiler_params=pltpu.CompilerParams(vmem_limit_bytes=40 << 20),
        name="factor",
    )(where, packed, own)


LAG, LAG2, STEPS = 2, 4, CELLS


def update_kernel(
    panel, front, pieces, held, rest, chunk, rest_sem,
    dsend, drecv, asend, arecv, bsend, brecv, xsend, xrecv, keep_sem,
):
    frame, cell = lax.axis_index("frame"), lax.axis_index("cell")
    x, core = frame // 2, lax.rem(frame, 2)
    y, z = cell // SIDE, lax.rem(cell, SIDE)
    right = lax.rem(x + 1, SIDE) * 2 + core
    left = lax.rem(x + SIDE - 1, SIDE) * 2 + core
    across = lax.rem(x + 2, SIDE) * 2 + core
    sibling = x * 2 + 1 - core
    has_rows = cell >= PB
    load = pltpu.make_async_copy(front.at[:, pl.ds(WIDTH, CELLS * BLK - WIDTH)], rest, rest_sem)

    @pl.when(has_rows)
    def _():
        load.start()

    held[cell] = panel[...]

    def row_peer(i):
        return y * SIDE + lax.rem(z + i, SIDE)

    def col_peer(i):
        return lax.rem(y + i, SIDE) * SIDE + z

    greet(
        [(frame, row_peer(i)) for i in range(1, SIDE)]
        + [(frame, col_peer(i)) for i in range(1, SIDE)]
        + [(left, cell), (right, cell), (sibling, cell)]
    )

    def direct(slot, src, to):
        return remote(held.at[src], held.at[src], dsend.at[slot], drecv.at[src], frame, to)

    def half_a(slot, src, to):
        part = held.at[src, pl.ds(0, 128)]
        return remote(part, part, asend.at[slot], arecv.at[src], frame, to)

    def half_b(slot, src, to):
        part = held.at[src, pl.ds(128, 128)]
        return remote(part, part, bsend.at[slot], brecv.at[src], frame, to)

    @pl.when(has_rows)
    def _():
        for i in (1, 3, 2):
            direct(i - 1, cell, row_peer(i)).start()
            direct(i + 2, cell, col_peer(i)).start()

    def order(t):
        i, by_row = 1 + (t - 1) // 2, lax.rem(t - 1, 2) == 0
        u = t - 7
        dy = jnp.where(t == 0, 0, jnp.where(t < 7, jnp.where(by_row, 0, i), 1 + u // 3))
        dz = jnp.where(t == 0, 0, jnp.where(t < 7, jnp.where(by_row, i, 0), 1 + lax.rem(u, 3)))
        return lax.rem(y + dy, SIDE) * SIDE + lax.rem(z + dz, SIDE)

    def x_copy(kind, c):
        whole = pl.ds(0, BLK)
        source, rows, to = [
            (frame, whole, right), (frame, whole, left), (frame, whole, sibling),
            (left, pl.ds(0, 128), right), (left, whole, sibling),
            (right, pl.ds(128, 128), left), (right, whole, sibling),
            (across, whole, sibling),
        ][kind]
        dst = pieces.at[source, c, rows]
        src = chunk.at[c, rows] if kind < 3 else dst
        return remote(src, dst, xsend.at[kind, c], xrecv.at[kind, c], to, cell)

    def keep(c):
        return pltpu.make_async_copy(chunk.at[c], pieces.at[frame, c], keep_sem.at[c])

    def step(t, carry):
        c = order(t)

        @pl.when((t < STEPS) & (c >= PB))
        def _():
            by_row = lax.rem(t - 1, 2) == 0

            @pl.when((t >= 1) & (t < 7))
            def _():
                direct(0, c, cell).wait_recv()

                @pl.when(by_row)
                def _():
                    for i in (1, 3, 2):
                        @pl.when(col_peer(i) >= PB)
                        def _(i=i):
                            half_a((t - 1) // 2 * 3 + i - 1, c, col_peer(i)).start()

                @pl.when(jnp.logical_not(by_row))
                def _():
                    for i in (1, 3, 2):
                        @pl.when(row_peer(i) >= PB)
                        def _(i=i):
                            half_b((t - 1) // 2 * 3 + i - 1, c, row_peer(i)).start()

            @pl.when(has_rows)
            def _():
                @pl.when(t == 0)
                def _():
                    load.wait()

                @pl.when(t >= 7)
                def _():
                    half_a(0, c, cell).wait_recv()
                    half_b(0, c, cell).wait_recv()

                product = lax.dot_general(panel[...], held[c], NT, preferred_element_type=F32)
                base = rest[:, pl.ds(pl.multiple_of((c - PB) * BLK, BLK), BLK)]
                chunk[c] = (base - product).astype(BF16)
                keep(c).start()
                for kind in range(3):
                    x_copy(kind, c).start()

        back = order(t - LAG)

        @pl.when((t >= LAG) & (t < STEPS + LAG) & has_rows & (back >= PB))
        def _():
            recv(0, left, pl.ds(0, BLK), back)
            x_copy(3, back).start()
            x_copy(4, back).start()
            recv(1, right, pl.ds(0, BLK), back)
            x_copy(5, back).start()
            x_copy(6, back).start()

        far = order(t - LAG2)

        @pl.when((t >= LAG2) & has_rows & (far >= PB))
        def _():
            recv(3, across, pl.ds(0, 128), far)
            recv(5, across, pl.ds(128, 128), far)
            x_copy(7, far).start()

        return carry

    def recv(kind, source, rows, c):
        dst = pieces.at[source, c, rows]
        remote(dst, dst, xsend.at[kind, c], xrecv.at[kind, c], sibling, cell).wait_recv()

    lax.fori_loop(0, STEPS + LAG2, step, 0)

    def finish(t, carry):
        @pl.when(has_rows & (t >= PB))
        def _():
            whole = pl.ds(0, BLK)
            recv(2, sibling, whole, t)
            other = 1 - 2 * core
            recv(4, left + other, whole, t)
            recv(6, right + other, whole, t)
            recv(7, across + other, whole, t)
            keep(t).wait()
            for kind in range(8):
                x_copy(kind, t).wait_send()

        return carry

    lax.fori_loop(0, CELLS, finish, 0)

    @pl.when(has_rows)
    def _():
        for i in range(1, SIDE):
            direct(i - 1, cell, row_peer(i)).wait_send()
            direct(i + 2, cell, col_peer(i)).wait_send()

    for k in range(SIDE - 1):
        for i in range(1, SIDE):
            @pl.when((row_peer(k + 1) >= PB) & (col_peer(i) >= PB))
            def _(k=k, i=i):
                half_a(k * 3 + i - 1, row_peer(k + 1), col_peer(i)).wait_send()

            @pl.when((col_peer(k + 1) >= PB) & (row_peer(i) >= PB))
            def _(k=k, i=i):
                half_b(k * 3 + i - 1, col_peer(k + 1), row_peer(i)).wait_send()


def update(panel, front):
    return pl.pallas_call(
        update_kernel,
        out_shape=jax.ShapeDtypeStruct((FRAMES, CELLS, BLK, BLK), BF16),
        in_specs=[pl.BlockSpec(memory_space=VMEM), pl.BlockSpec(memory_space=pl.ANY)],
        out_specs=pl.BlockSpec(memory_space=pl.ANY),
        scratch_shapes=[
            VMEM((CELLS, BLK, WIDTH), BF16),
            VMEM((BLK, CELLS * BLK - WIDTH), F32),
            VMEM((CELLS, BLK, BLK), BF16),
            DMA,
            DMA((6,)), DMA((CELLS,)), DMA((9,)), DMA((CELLS,)), DMA((9,)), DMA((CELLS,)),
            DMA((8, CELLS)), DMA((8, CELLS)), DMA((CELLS,)),
        ],
        compiler_params=pltpu.CompilerParams(
            collective_id=2, has_side_effects=True, vmem_limit_bytes=40 << 20
        ),
        name="update",
    )(panel, front)


GROUP = 4
SPAN = GROUP * BLK


def extend_kernel(half_ref, side_ref, parent, pieces, out, total):
    q, g = pl.program_id(0), pl.program_id(1)
    total[...] = parent[...].astype(F32)
    for c in range(FRAMES):
        half = half_ref[c]

        @pl.when(half >= 0)
        def _(c=c, half=half):
            for i in range(GROUP):
                block = q * GROUP + i

                @pl.when((block >= PB) & (side_ref[c * CELLS + block] == g))
                def _(i=i):
                    total[half, :, i * BLK:(i + 1) * BLK] += pieces[c, i].astype(F32)

    out[...] = total[...].astype(BF16)


def extend(half, side, parent, pieces):
    whole = CELLS // GROUP
    return pl.pallas_call(
        extend_kernel,
        out_shape=jax.ShapeDtypeStruct(parent.shape, BF16),
        grid_spec=pltpu.PrefetchScalarGridSpec(
            num_scalar_prefetch=2,
            grid=(whole, 2),
            in_specs=[
                pl.BlockSpec((2, BLK, SPAN), lambda q, g, h, s: (0, 0, g * whole + q)),
                pl.BlockSpec((FRAMES, GROUP, BLK, BLK), lambda q, g, h, s: (0, q, 0, 0)),
            ],
            out_specs=pl.BlockSpec((2, BLK, SPAN), lambda q, g, h, s: (0, 0, g * whole + q)),
            scratch_shapes=[VMEM((2, BLK, SPAN), F32)],
        ),
        compiler_params=pltpu.CompilerParams(vmem_limit_bytes=40 << 20),
        name="extend",
    )(half, side, parent, pieces)


def per_device(front, parent_of, block_map, parent_in):
    rows = front[0]
    cell, frame = lax.axis_index("cell"), lax.axis_index("frame")
    packed = gather_pivot(rows).reshape(BLK, PACKED)
    start = jnp.where(cell < PB, cell * BLK, WIDTH).astype(jnp.int32)[None]
    lower, panel = factor(start, packed, rows[:, :WIDTH])
    pieces = update(panel, rows)
    upper = block_map // CELLS
    mine = lax.dynamic_index_in_dim(upper, jnp.maximum(cell - PB, 0), 1, keepdims=False)
    half = jnp.where((parent_of == frame) & (cell >= PB), mine, -1).astype(jnp.int32)
    side = jnp.pad(upper, ((0, 0), (PB, 0))).reshape(-1).astype(jnp.int32)
    out = extend(half, side, parent_in[0], pieces)
    return lower[None], out[None]


def solution(mesh):
    placed = (P("frame", "cell", None), P(), P(), P("frame", None, "cell", None))
    return jax.shard_map(
        per_device,
        mesh=mesh,
        in_specs=placed,
        out_specs=(P("frame", "cell", None), P("frame", None, "cell", None)),
        check_vma=False,
    )
```

```python
import functools

import jax
import jax.numpy as jnp
from jax import lax
from jax.experimental import pallas as pl
from jax.experimental.pallas import tpu as pltpu
from jax.sharding import PartitionSpec as P

PB = 3
BLK = 256
F32, BF16 = jnp.float32, jnp.bfloat16
NT = (((1,), (1,)), ((), ()))
TN = (((0,), (0,)), ((), ()))
STRIP = 16
SIDE = 4
CELLS = SIDE * SIDE
FRAMES = 2 * SIDE
WIDTH = PB * BLK
VMEM = pltpu.VMEM
DMA = pltpu.SemaphoreType.DMA
MESH = pl.DeviceIdType.MESH


def remote(src, dst, send, recv, frame, cell):
    return pltpu.make_async_remote_copy(
        src_ref=src, dst_ref=dst, send_sem=send, recv_sem=recv,
        device_id=(frame, cell), device_id_type=MESH,
    )


def greet(devices):
    barrier = pltpu.get_barrier_semaphore()
    for frame, cell in devices:
        pl.semaphore_signal(barrier, inc=1, device_id=(frame, cell), device_id_type=MESH)
    pl.semaphore_wait(barrier, len(devices))


def split(x):
    hi = x.astype(BF16)
    return hi, (x - hi.astype(F32)).astype(BF16)


def dot3(a, b, dims):
    def one(u, v):
        return lax.dot_general(u, v, dims, preferred_element_type=F32)

    return one(a[0], b[0]) + one(a[0], b[1]) + one(a[1], b[0])


def strip_step(s, work, done):
    first = pl.multiple_of(s * STRIP, STRIP)
    rows = work[pl.ds(first, STRIP), :]
    left, right = rows[:, :128], rows[:, 128:]
    turned = pltpu.roll(left, lax.rem(128 - first, 128), 1)
    cols = [jnp.broadcast_to(turned[:, b:b + 1], (STRIP, 128)) for b in range(STRIP)]
    row_no = lax.broadcasted_iota(jnp.int32, (STRIP, 128), 0)
    lane = lax.broadcasted_iota(jnp.int32, (STRIP, 128), 1)
    scale = jnp.zeros((STRIP, 128), F32)
    for a in range(STRIP):
        below = jnp.where(row_no > a, cols[a], 0.0)
        root = jnp.broadcast_to(lax.rsqrt(cols[a][a:a + 1, :]), (STRIP, 128))
        over = root * root
        scale = jnp.where(row_no == a, root, scale)
        if a < STRIP - 1:
            for b in range(a + 1, STRIP):
                cols[b] = cols[b] - (below * cols[b][a:a + 1, :]) * over
            ratio = below * over
            left = left - ratio * left[a:a + 1, :]
            right = right - ratio * right[a:a + 1, :]
    upper = jnp.where(lane >= row_no + first, left * scale, 0.0)
    inverse = right * scale
    done[pl.ds(first, STRIP), :128] = upper
    done[pl.ds(first, STRIP), 128:] = inverse
    u1, u2 = split(upper)
    v1, v2 = split(inverse)
    one, two = jnp.concatenate([u1, v1], 1), jnp.concatenate([u2, v2], 1)
    work[...] -= lax.dot_general(
        jnp.concatenate([u1, u1, u2], 0), jnp.concatenate([one, two, one], 0), TN,
        preferred_element_type=F32,
    )


LAG, LAG2, STEPS = 2, 4, CELLS
HALF = BLK // 2
ORDER = (1, 3, 2)


def fronts_kernel(
    front, lower, pieces,
    raw, a, a_hi, a_lo, own, own_hi, own_lo, inv_hi, inv_lo, work, done,
    stage_a, stage_b, held, rest, chunk,
    load_sem, s1_send, s1_recv, s1_keep, s2_send, s2_recv,
    d_send, d_recv, f_send, f_recv, l_send, l_recv, h_send, h_recv,
    x_send, x_recv, keep_sem,
):
    frame, cell = lax.axis_index("frame"), lax.axis_index("cell")
    x, core = frame // 2, lax.rem(frame, 2)
    y, z = cell // SIDE, lax.rem(cell, SIDE)
    right = lax.rem(x + 1, SIDE) * 2 + core
    left = lax.rem(x + SIDE - 1, SIDE) * 2 + core
    across = lax.rem(x + 2, SIDE) * 2 + core
    sibling = x * 2 + 1 - core
    has_rows = cell >= PB

    def row_peer(i):
        return y * SIDE + lax.rem(z + i, SIDE)

    def col_peer(i):
        return lax.rem(y + i, SIDE) * SIDE + z

    load_own = pltpu.make_async_copy(front.at[:, pl.ds(0, WIDTH)], own, load_sem.at[0])
    load_rest = pltpu.make_async_copy(
        front.at[:, pl.ds(WIDTH, CELLS * BLK - WIDTH)], rest, load_sem.at[1]
    )
    greet(
        [(frame, row_peer(i)) for i in range(1, SIDE)]
        + [(frame, col_peer(i)) for i in range(1, SIDE)]
        + [(left, cell), (right, cell), (sibling, cell)]
    )

    def stage_copy(r, kind, i):
        wide = pl.ds(0, BLK * (r + 1))
        if kind == 0:
            to, first, buffer = lax.rem(r + i, SIDE), 32 * ((r + i) % SIDE), stage_a
        else:
            to, first, buffer = i * SIDE + r, HALF + 32 * i, stage_b
        src, dst = front.at[pl.ds(first, 32), wide], buffer.at[r, :, wide]
        if i == 0:
            return pltpu.make_async_copy(src, dst, s1_keep.at[kind])
        return remote(src, dst, s1_send.at[kind, i], s1_recv.at[kind, r], frame, to)

    def region(r, kind, ys, zs):
        if kind == 0:
            first = BLK * r + 32 * zs + 8 * ys
        else:
            first = BLK * r + HALF + 32 * ys + 8 * zs
        return raw.at[pl.ds(pl.multiple_of(first, 8), 8), pl.ds(0, BLK * (r + 1))]

    def part_copy(r, kind, i):
        wide = pl.ds(0, BLK * (r + 1))
        if kind == 0:
            at = lax.rem(y + i, SIDE)
            to, dst, buffer = col_peer(i), region(r, 0, at, z), stage_a
        else:
            at = lax.rem(z + i, SIDE)
            to, dst, buffer = row_peer(i), region(r, 1, y, at), stage_b
        src = buffer.at[r, pl.ds(pl.multiple_of(8 * at, 8), 8), wide]
        if i == 0:
            return src, dst
        return remote(src, dst, s2_send.at[r, kind, i], s2_recv.at[r, kind], frame, to)

    def to_peer(r, kind, slot, to):
        part = region(r, kind, y, z)
        return remote(part, part, d_send.at[r, kind, slot], d_recv.at[r, kind, cell], frame, to)

    def from_peer(r, kind, ys, zs):
        part, src = region(r, kind, ys, zs), ys * SIDE + zs
        remote(part, part, d_send.at[r, kind, 0], d_recv.at[r, kind, src], frame, src).wait_recv()

    def forward(r, kind, slot, ys, zs, to):
        part, src = region(r, kind, ys, zs), ys * SIDE + zs
        return remote(part, part, f_send.at[r, kind, slot], f_recv.at[r, kind, src], frame, to)

    def pivot_start():
        for r in range(PB):
            @pl.when(cell == r)
            def _(r=r):
                for i in (0,) + ORDER:
                    for kind in range(2):
                        stage_copy(r, kind, i).start()

    def pivot_parts(r):
        for kind, holds in ((0, y == 0), (1, z == r)):
            @pl.when(holds)
            def _(kind=kind):
                @pl.when(cell == r)
                def _():
                    stage_copy(r, kind, 0).wait()

                @pl.when(cell != r)
                def _():
                    stage_copy(r, kind, 1).wait_recv()

                for i in ORDER:
                    part_copy(r, kind, i).start()
                src, dst = part_copy(r, kind, 0)
                dst[...] = src[...]

            @pl.when(jnp.logical_not(holds))
            def _(kind=kind):
                part = region(r, kind, y, z)
                remote(part, part, s2_send.at[r, kind, 0], s2_recv.at[r, kind], frame, cell).wait_recv()

        for i in ORDER:
            for kind in range(2):
                to_peer(r, kind, i - 1, row_peer(i)).start()
                to_peer(r, kind, i + 2, col_peer(i)).start()

    def pivot_forward(r):
        for i in ORDER:
            zs, ys = lax.rem(z + i, SIDE), lax.rem(y + i, SIDE)
            from_peer(r, 0, y, zs)
            for k in ORDER:
                forward(r, 0, (i - 1) * 3 + k - 1, y, zs, col_peer(k)).start()
            from_peer(r, 1, ys, z)
            for k in ORDER:
                forward(r, 1, (i - 1) * 3 + k - 1, ys, z, row_peer(k)).start()
        for i in ORDER:
            from_peer(r, 1, y, lax.rem(z + i, SIDE))
            from_peer(r, 0, lax.rem(y + i, SIDE), z)

    def pivot_end(r):
        for i in ORDER:
            for k in ORDER:
                ys, zs = lax.rem(y + i, SIDE), lax.rem(z + k, SIDE)
                for kind in range(2):
                    forward(r, kind, 0, ys, zs, cell).wait_recv()

    def pivot_sent(r):
        @pl.when(cell == r)
        def _():
            for i in ORDER:
                for kind in range(2):
                    stage_copy(r, kind, i).wait_send()

        for kind, holds in ((0, y == 0), (1, z == r)):
            @pl.when(holds)
            def _(kind=kind):
                for i in ORDER:
                    part_copy(r, kind, i).wait_send()

            for i in ORDER:
                to_peer(r, kind, i - 1, row_peer(i)).wait_send()
                to_peer(r, kind, i + 2, col_peer(i)).wait_send()
                for k in ORDER:
                    slot = (i - 1) * 3 + k - 1
                    if kind == 0:
                        forward(r, 0, slot, y, lax.rem(z + i, SIDE), col_peer(k)).wait_send()
                    else:
                        forward(r, 1, slot, lax.rem(y + i, SIDE), z, row_peer(k)).wait_send()

    def panel_step(source, full, hi, lo, first, count, j):
        rows, here = pl.ds(first, count), pl.ds(128 * j, 128)
        value = source[rows, here]
        if j > 0:
            past = pl.ds(0, 128 * j)
            value = value - dot3((hi[rows, past], lo[rows, past]), (a_hi[here, past], a_lo[here, past]), NT)
        value = dot3(split(value), (inv_hi[j], inv_lo[j]), NT)
        full[rows, here] = value
        hi[rows, here], lo[rows, here] = split(value)

    def pivot_step(j):
        here, past = pl.ds(128 * j, 128), pl.ds(0, 128 * j)
        value = raw[here, here]
        if j > 0:
            both = a_hi[here, past], a_lo[here, past]
            value = value - dot3(both, both, NT)
        work[:, :128] = value
        work[:, 128:] = (
            lax.broadcasted_iota(jnp.int32, (128, 128), 0)
            == lax.broadcasted_iota(jnp.int32, (128, 128), 1)
        ).astype(F32)

        def step(s, carry):
            strip_step(s, work, done)
            return carry

        lax.fori_loop(0, 128 // STRIP, step, 0)
        inv_hi[j], inv_lo[j] = split(done[:, 128:])
        a[here, here] = done[:, :128].T

    def panel_to(q, slot, to):
        block = held.at[q, cell]
        return remote(block, block, l_send.at[q, slot], l_recv.at[q, cell], frame, to)

    def half_block(q, kind, src):
        return held.at[q, src, pl.ds(HALF * kind, HALF)]

    def half_to(q, kind, slot, src, to):
        block = half_block(q, kind, src)
        return remote(block, block, h_send.at[q, kind, slot], h_recv.at[q, kind, src], frame, to)

    def own_step(q):
        @pl.when(has_rows)
        def _():
            panel_step(own, own, own_hi, own_lo, 0, BLK, 2 * q)
            panel_step(own, own, own_hi, own_lo, 0, BLK, 2 * q + 1)
            held[q, cell] = own_hi[:, BLK * q:BLK * (q + 1)]
            for i in ORDER:
                panel_to(q, i - 1, row_peer(i)).start()
                panel_to(q, i + 2, col_peer(i)).start()

    def panel_forward(q, i, by_row, act):
        src = row_peer(i) if by_row else col_peer(i)

        @pl.when(src >= PB)
        def _():
            if act == "start":
                block = held.at[q, src]
                remote(block, block, l_send.at[q, 0], l_recv.at[q, src], frame, src).wait_recv()
            for k in ORDER:
                to = col_peer(k) if by_row else row_peer(k)

                @pl.when(to >= PB)
                def _(to=to, k=k):
                    copy = half_to(q, 0 if by_row else 1, (i - 1) * 3 + k - 1, src, to)
                    copy.start() if act == "start" else copy.wait_send()

    pivot_start()
    load_own.start()

    @pl.when(has_rows)
    def _():
        load_rest.start()

    pivot_parts(0)
    pivot_forward(0)
    pivot_parts(1)
    pivot_end(0)
    load_own.wait()
    pivot_step(0)
    pivot_forward(1)
    panel_step(raw, a, a_hi, a_lo, 128, 128, 0)
    pivot_step(1)
    pivot_parts(2)
    own_step(0)
    pivot_end(1)
    for j in range(2):
        panel_step(raw, a, a_hi, a_lo, BLK, BLK, j)
    pivot_step(2)
    pivot_forward(2)
    panel_step(raw, a, a_hi, a_lo, 384, 128, 2)
    pivot_step(3)
    own_step(1)
    for i in ORDER:
        panel_forward(0, i, True, "start")
        panel_forward(0, i, False, "start")
    pivot_end(2)
    for j in range(4):
        panel_step(raw, a, a_hi, a_lo, 2 * BLK, BLK, j)
    pivot_step(4)
    panel_step(raw, a, a_hi, a_lo, 640, 128, 4)
    pivot_step(5)
    own_step(2)
    for i in ORDER:
        panel_forward(1, i, True, "start")
        panel_forward(1, i, False, "start")

    def order(t):
        pair, by_row = (t - 1) // 2, lax.rem(t - 1, 2) == 0
        i = jnp.where(pair == 0, 1, jnp.where(pair == 1, 3, 2))
        u = t - 7
        dy = jnp.where(t == 0, 0, jnp.where(t < 7, jnp.where(by_row, 0, i), 1 + u // 3))
        dz = jnp.where(t == 0, 0, jnp.where(t < 7, jnp.where(by_row, i, 0), 1 + lax.rem(u, 3)))
        return lax.rem(y + dy, SIDE) * SIDE + lax.rem(z + dz, SIDE)

    whole = pl.ds(0, BLK)

    def x_copy(kind, c):
        source, rows, to = [
            (frame, whole, right), (frame, whole, left), (frame, whole, sibling),
            (left, pl.ds(0, HALF), right), (left, whole, sibling),
            (right, pl.ds(HALF, HALF), left), (right, whole, sibling),
            (across, whole, sibling),
        ][kind]
        dst = pieces.at[source, c, rows]
        src = chunk.at[c, rows] if kind < 3 else dst
        return remote(src, dst, x_send.at[kind, c], x_recv.at[kind, c], to, cell)

    def arrived(kind, source, rows, c):
        dst = pieces.at[source, c, rows]
        remote(dst, dst, x_send.at[kind, c], x_recv.at[kind, c], sibling, cell).wait_recv()

    def keep(c):
        return pltpu.make_async_copy(chunk.at[c], pieces.at[frame, c], keep_sem.at[c])

    def step(t, carry):
        c = order(t)
        for n, i in enumerate(ORDER):
            for by_row in (True, False):
                @pl.when(t == 1 + 2 * n + (0 if by_row else 1))
                def _(i=i, by_row=by_row):
                    panel_forward(2, i, by_row, "start")

        @pl.when((t < STEPS) & (c >= PB) & has_rows)
        def _():
            @pl.when(t == 0)
            def _():
                load_rest.wait()

            @pl.when(t >= 7)
            def _():
                for q in range(PB):
                    for kind in range(2):
                        half_to(q, kind, 0, c, cell).wait_recv()

            value = rest[:, pl.ds(pl.multiple_of((c - PB) * BLK, BLK), BLK)]
            for q in range(PB):
                value = value - lax.dot_general(
                    own_hi[:, BLK * q:BLK * (q + 1)], held[q, c], NT, preferred_element_type=F32
                )
            chunk[c] = value.astype(BF16)
            keep(c).start()
            for kind in range(3):
                x_copy(kind, c).start()

        back = order(t - LAG)

        @pl.when((t >= LAG) & (t < STEPS + LAG) & has_rows & (back >= PB))
        def _():
            arrived(0, left, whole, back)
            x_copy(3, back).start()
            x_copy(4, back).start()
            arrived(1, right, whole, back)
            x_copy(5, back).start()
            x_copy(6, back).start()

        far = order(t - LAG2)

        @pl.when((t >= LAG2) & has_rows & (far >= PB))
        def _():
            arrived(3, across, pl.ds(0, HALF), far)
            arrived(5, across, pl.ds(HALF, HALF), far)
            x_copy(7, far).start()

        return carry

    lax.fori_loop(0, STEPS + LAG2, step, 0)

    for r in range(PB):
        @pl.when(cell == r)
        def _(r=r):
            row_no = lax.broadcasted_iota(jnp.int32, (BLK, WIDTH), 0) + BLK * r
            col_no = lax.broadcasted_iota(jnp.int32, (BLK, WIDTH), 1)
            lower[...] = jnp.where(row_no >= col_no, a[BLK * r:BLK * (r + 1), :], 0.0)

    @pl.when(has_rows)
    def _():
        lower[...] = own[...]

    def finish(t, carry):
        @pl.when(has_rows & (t >= PB))
        def _():
            other = 1 - 2 * core
            arrived(2, sibling, whole, t)
            arrived(4, left + other, whole, t)
            arrived(6, right + other, whole, t)
            arrived(7, across + other, whole, t)
            keep(t).wait()
            for kind in range(8):
                x_copy(kind, t).wait_send()

        return carry

    for r in range(PB):
        pivot_sent(r)
    for q in range(PB):
        @pl.when(has_rows)
        def _(q=q):
            for i in ORDER:
                panel_to(q, i - 1, row_peer(i)).wait_send()
                panel_to(q, i + 2, col_peer(i)).wait_send()

        for i in ORDER:
            panel_forward(q, i, True, "end")
            panel_forward(q, i, False, "end")
    lax.fori_loop(0, CELLS, finish, 0)


def fronts(front):
    rest = CELLS * BLK - WIDTH
    return pl.pallas_call(
        fronts_kernel,
        out_shape=(
            jax.ShapeDtypeStruct((BLK, WIDTH), F32),
            jax.ShapeDtypeStruct((FRAMES, CELLS, BLK, BLK), BF16),
        ),
        in_specs=[pl.BlockSpec(memory_space=pl.ANY)],
        out_specs=(pl.BlockSpec(memory_space=VMEM), pl.BlockSpec(memory_space=pl.ANY)),
        scratch_shapes=[
            VMEM((WIDTH, WIDTH), F32), VMEM((WIDTH, WIDTH), F32),
            VMEM((WIDTH, WIDTH), BF16), VMEM((WIDTH, WIDTH), BF16),
            VMEM((BLK, WIDTH), F32), VMEM((BLK, WIDTH), BF16), VMEM((BLK, WIDTH), BF16),
            VMEM((WIDTH // 128, 128, 128), BF16), VMEM((WIDTH // 128, 128, 128), BF16),
            VMEM((128, 256), F32), VMEM((128, 256), F32),
            VMEM((PB, 32, WIDTH), F32), VMEM((PB, 32, WIDTH), F32),
            VMEM((PB, CELLS, BLK, BLK), BF16), VMEM((BLK, rest), F32), VMEM((CELLS, BLK, BLK), BF16),
            DMA((2,)), DMA((2, SIDE)), DMA((2, PB)), DMA((2,)), DMA((PB, 2, SIDE)), DMA((PB, 2)),
            DMA((PB, 2, 6)), DMA((PB, 2, CELLS)), DMA((PB, 2, 9)), DMA((PB, 2, CELLS)),
            DMA((PB, 6)), DMA((PB, CELLS)), DMA((PB, 2, 9)), DMA((PB, 2, CELLS)),
            DMA((8, CELLS)), DMA((8, CELLS)), DMA((CELLS,)),
        ],
        compiler_params=pltpu.CompilerParams(
            collective_id=1, has_side_effects=True, vmem_limit_bytes=56 << 20
        ),
        name="fronts",
    )(front)


GROUP = 4
SPAN = GROUP * BLK
WHOLE = CELLS // GROUP


def extend_kernel(parent_of, block_map, parent, pieces, out, total, buffer, sems):
    q, g = pl.program_id(0), pl.program_id(1)
    frame, cell = lax.axis_index("frame"), lax.axis_index("cell")
    turn = lax.rem(q, 2)

    def live(c):
        return (parent_of[c] == frame) & (cell >= PB)

    def fetch(c, at):
        slot = lax.rem(at, 2)
        return pltpu.make_async_copy(
            pieces.at[c, pl.ds(at * GROUP, GROUP)], buffer.at[slot, c], sems.at[slot, c]
        )

    for c in range(FRAMES):
        @pl.when(live(c) & (q == 0) & (g == 0))
        def _(c=c):
            fetch(c, q).start()

    for c in range(FRAMES):
        @pl.when(live(c) & (q + 1 < WHOLE) & (g == 0))
        def _(c=c):
            fetch(c, q + 1).start()

    total[...] = parent[...].astype(F32)
    for c in range(FRAMES):
        @pl.when(live(c))
        def _(c=c):
            half = block_map[c, jnp.maximum(cell - PB, 0)] // CELLS

            @pl.when(g == 0)
            def _():
                fetch(c, q).wait()

            for i in range(GROUP):
                block = q * GROUP + i

                @pl.when((block >= PB) & (block_map[c, jnp.maximum(block - PB, 0)] // CELLS == g))
                def _(i=i):
                    total[half, :, i * BLK:(i + 1) * BLK] += buffer[turn, c, i].astype(F32)

    out[...] = total[...].astype(BF16)


def extend(parent_of, block_map, parent, pieces):
    tile = pl.BlockSpec((2, BLK, SPAN), lambda q, g, *_: (0, 0, g * WHOLE + q))
    return pl.pallas_call(
        extend_kernel,
        out_shape=jax.ShapeDtypeStruct(parent.shape, BF16),
        grid_spec=pltpu.PrefetchScalarGridSpec(
            num_scalar_prefetch=2,
            grid=(WHOLE, 2),
            in_specs=[tile, pl.BlockSpec(memory_space=pl.ANY)],
            out_specs=tile,
            scratch_shapes=[
                VMEM((2, BLK, SPAN), F32), VMEM((2, FRAMES, GROUP, BLK, BLK), BF16), DMA((2, FRAMES)),
            ],
        ),
        compiler_params=pltpu.CompilerParams(vmem_limit_bytes=60 << 20),
        name="extend",
    )(parent_of, block_map, parent, pieces)


def per_device(front, parent_of, block_map, parent_in):
    lower, pieces = fronts(front[0])
    out = extend(parent_of, block_map, parent_in[0], pieces)
    return lower[None], out[None]


def solution(mesh):
    placed = (P("frame", "cell", None), P(), P(), P("frame", None, "cell", None))
    return jax.shard_map(
        per_device,
        mesh=mesh,
        in_specs=placed,
        out_specs=(P("frame", "cell", None), P("frame", None, "cell", None)),
        check_vma=False,
    )
```

```python
import functools

import jax
import jax.numpy as jnp
from jax import lax
from jax.experimental import pallas as pl
from jax.experimental.pallas import tpu as pltpu
from jax.sharding import PartitionSpec as P

PB = 3
BLK = 256
F32, BF16 = jnp.float32, jnp.bfloat16
NT = (((1,), (1,)), ((), ()))
TN = (((0,), (0,)), ((), ()))
STRIP = 16
SIDE = 4
CELLS = SIDE * SIDE
FRAMES = 2 * SIDE
WIDTH = PB * BLK
VMEM = pltpu.VMEM
DMA = pltpu.SemaphoreType.DMA
MESH = pl.DeviceIdType.MESH


def remote(src, dst, send, recv, frame, cell):
    return pltpu.make_async_remote_copy(
        src_ref=src, dst_ref=dst, send_sem=send, recv_sem=recv,
        device_id=(frame, cell), device_id_type=MESH,
    )


def greet(devices):
    barrier = pltpu.get_barrier_semaphore()
    for frame, cell in devices:
        pl.semaphore_signal(barrier, inc=1, device_id=(frame, cell), device_id_type=MESH)
    pl.semaphore_wait(barrier, len(devices))


def split(x):
    hi = x.astype(BF16)
    return hi, (x - hi.astype(F32)).astype(BF16)


def dot3(a, b, dims):
    def one(u, v):
        return lax.dot_general(u, v, dims, preferred_element_type=F32)

    return one(a[0], b[0]) + one(a[0], b[1]) + one(a[1], b[0])


def strip_static(s, work, done):
    first = STRIP * s
    left_t, left_b = work[first:first + 8, :128], work[first + 8:first + 16, :128]
    right_t, right_b = work[first:first + 8, 128:], work[first + 8:first + 16, 128:]
    spread = lambda v, b: jnp.broadcast_to(v[:, first + b:first + b + 1], (8, 128))
    pick = lambda v, a: jnp.broadcast_to(v[a:a + 1, :], (8, 128))
    cols_t = [spread(left_t, b) for b in range(STRIP)]
    cols_b = [spread(left_b, b) for b in range(STRIP)]
    row_no = lax.broadcasted_iota(jnp.int32, (8, 128), 0)
    lane = lax.broadcasted_iota(jnp.int32, (8, 128), 1)
    scale_t = scale_b = jnp.zeros((8, 128), F32)
    for a in range(8):
        root = lax.rsqrt(pick(cols_t[a], a))
        over = root * root
        scale_t = jnp.where(row_no == a, root, scale_t)
        ratio_t = jnp.where(row_no > a, cols_t[a], 0.0) * over
        ratio_b = cols_b[a] * over
        for b in range(a + 1, STRIP):
            here = pick(cols_t[b], a)
            if a < 7:
                cols_t[b] = cols_t[b] - ratio_t * here
            cols_b[b] = cols_b[b] - ratio_b * here
        l, r = pick(left_t, a), pick(right_t, a)
        left_t, right_t = left_t - ratio_t * l, right_t - ratio_t * r
        left_b, right_b = left_b - ratio_b * l, right_b - ratio_b * r
    for a in range(8):
        root = lax.rsqrt(pick(cols_b[8 + a], a))
        scale_b = jnp.where(row_no == a, root, scale_b)
        if a == 7:
            break
        ratio_b = jnp.where(row_no > a, cols_b[8 + a], 0.0) * (root * root)
        for b in range(9 + a, STRIP):
            cols_b[b] = cols_b[b] - ratio_b * pick(cols_b[b], a)
        l, r = pick(left_b, a), pick(right_b, a)
        left_b, right_b = left_b - ratio_b * l, right_b - ratio_b * r
    up = jnp.concatenate([
        jnp.where(lane >= row_no + first, left_t * scale_t, 0.0),
        jnp.where(lane >= row_no + first + 8, left_b * scale_b, 0.0)], 0)
    inv = jnp.concatenate([right_t * scale_t, right_b * scale_b], 0)
    done[first:first + STRIP, :128] = up
    done[first:first + STRIP, 128:] = inv
    end = first + STRIP
    if end < 128:
        u1, u2 = split(up)
        v1, v2 = split(inv)
        lhs = jnp.concatenate([u1, u1, u2], 0)
        one, two = jnp.concatenate([u1, v1], 1), jnp.concatenate([u2, v2], 1)
        rhs = jnp.concatenate([one, two, one], 0)
        work[end:, :] -= lax.dot_general(lhs, rhs, TN, preferred_element_type=F32)[end:]


LAG, LAG2, STEPS = 5, 10, CELLS
HALF = BLK // 2
ORDER = (1, 3, 2)
PANELS = ((0, 256), (256, 256), (512, 128), (640, 128))


def fronts_kernel(
    front, lower, pieces,
    raw, a, a_hi, a_lo, own, own_hi, own_lo, inv_hi, inv_lo, work, done,
    held, rest, chunk,
    load_sem, s1_send, s1_recv, s1_keep, s2_send, s2_recv, s3_send, s3_recv,
    l_send, l_recv, h_send, h_recv,
    x_send, near, far_sem, late, keep_sem,
):
    frame, cell = lax.axis_index("frame"), lax.axis_index("cell")
    x, core = frame // 2, lax.rem(frame, 2)
    y, z = cell // SIDE, lax.rem(cell, SIDE)
    right = lax.rem(x + 1, SIDE) * 2 + core
    left = lax.rem(x + SIDE - 1, SIDE) * 2 + core
    across = lax.rem(x + 2, SIDE) * 2 + core
    sibling = x * 2 + 1 - core
    has_rows = cell >= PB

    def row_peer(i):
        return y * SIDE + lax.rem(z + i, SIDE)

    def col_peer(i):
        return lax.rem(y + i, SIDE) * SIDE + z

    load_own = pltpu.make_async_copy(front.at[:, pl.ds(0, WIDTH)], own, load_sem.at[0])
    load_rest = pltpu.make_async_copy(
        front.at[:, pl.ds(WIDTH, CELLS * BLK - WIDTH)], rest, load_sem.at[1]
    )
    greet(
        [(frame, row_peer(i)) for i in range(1, SIDE)]
        + [(frame, col_peer(i)) for i in range(1, SIDE)]
        + [(left, cell), (right, cell), (sibling, cell)]
    )

    def quarter(r, kind, at):
        first = pl.multiple_of(BLK * r + HALF * kind + 32 * at, 32)
        return raw.at[pl.ds(first, 32), pl.ds(0, BLK * r + 128 * (kind + 1))]

    def place(kind):
        return z if kind == 0 else y

    def along(kind, i):
        return row_peer(i) if kind == 0 else col_peer(i)

    def first_copy(r, kind, i):
        at = (r + i) % SIDE if kind == 0 else i
        src = front.at[pl.ds(HALF * kind + 32 * at, 32), pl.ds(0, BLK * r + 128 * (kind + 1))]
        if i == 0:
            return pltpu.make_async_copy(src, quarter(r, kind, at), s1_keep.at[kind])
        return remote(
            src, quarter(r, kind, at), s1_send.at[0], s1_recv.at[kind, r], frame,
            at if kind == 0 else at * SIDE + r,
        )

    def second_copy(r, kind, i):
        part = quarter(r, kind, place(kind))
        return remote(part, part, s2_send.at[r, kind], s2_recv.at[r, kind], frame, along(1 - kind, i))

    def third_copy(r, kind, i):
        part = quarter(r, kind, place(kind))
        return remote(
            part, part, s3_send.at[r, kind], s3_recv.at[r], frame, along(kind, i)
        )

    def pivot_start():
        for r in range(PB):
            @pl.when(cell == r)
            def _(r=r):
                for i in (0,) + ORDER:
                    for kind in range(2):
                        first_copy(r, kind, i).start()

    def pivot_send(r):
        for kind, holds in ((0, y == 0), (1, z == r)):
            @pl.when(holds)
            def _(kind=kind):
                @pl.when(cell == r)
                def _():
                    first_copy(r, kind, 0).wait()

                @pl.when(cell != r)
                def _():
                    part = quarter(r, kind, place(kind))
                    remote(part, part, s1_send.at[0], s1_recv.at[kind, r], frame, cell).wait_recv()

                for i in ORDER:
                    second_copy(r, kind, i).start()

            @pl.when(jnp.logical_not(holds))
            def _(kind=kind):
                second_copy(r, kind, 0).wait_recv()

            for i in ORDER:
                third_copy(r, kind, i).start()

    def six(r):
        return raw.at[pl.ds(0, 32 * (4 * r + 3)), pl.ds(0, 384)]

    def pivot_end(r):
        part = six(r)
        remote(part, part, s3_send.at[r, 0], s3_recv.at[r], frame, cell).wait_recv()

    def pivot_sent(r):
        @pl.when(cell == r)
        def _():
            part = six(r)
            remote(part, part, s1_send.at[0], s1_recv.at[0, r], frame, cell).wait_send()

        for kind, holds in ((0, y == 0), (1, z == r)):
            part = raw.at[pl.ds(0, 3 * 32), pl.ds(0, BLK * r + 128 * (kind + 1))]

            @pl.when(holds)
            def _(kind=kind, part=part):
                remote(part, part, s2_send.at[r, kind], s2_recv.at[r, kind], frame, cell).wait_send()

            remote(part, part, s3_send.at[r, kind], s3_recv.at[r], frame, cell).wait_send()

    def panel_step(source, full, hi, lo, first, count, j):
        rows, here = pl.ds(first, count), pl.ds(128 * j, 128)
        value = source[rows, here]
        if j > 0:
            past = pl.ds(0, 128 * j)
            value = value - dot3((hi[rows, past], lo[rows, past]), (a_hi[here, past], a_lo[here, past]), NT)
        value = dot3(split(value), (inv_hi[j], inv_lo[j]), NT)
        full[rows, here] = value
        hi[rows, here], lo[rows, here] = split(value)

    def pivot_step(j):
        here, past = pl.ds(128 * j, 128), pl.ds(0, 128 * j)
        value = raw[here, here]
        if j > 0:
            both = a_hi[here, past], a_lo[here, past]
            value = value - dot3(both, both, NT)
        work[:, :128] = value
        work[:, 128:] = (
            lax.broadcasted_iota(jnp.int32, (128, 128), 0)
            == lax.broadcasted_iota(jnp.int32, (128, 128), 1)
        ).astype(F32)

        for s in range(128 // STRIP):
            strip_static(s, work, done)
        inv_hi[j], inv_lo[j] = split(done[:, 128:])
        a[here, here] = done[:, :128].T

    def block(q, src, first, count):
        start, wide = PANELS[q]
        return held.at[start // BLK, src, pl.ds(first, count), pl.ds(start % BLK, wide)]

    def panel_to(q, i, by_row):
        to, slot = (row_peer(i), 3 - i) if by_row else (col_peer(i), 6 - i)
        part = block(q, cell, 0, BLK)
        return remote(part, part, l_send.at[q], l_recv.at[q, slot], frame, to)

    def half_to(q, kind, src, to):
        part = block(q, src, HALF * kind, HALF)
        return remote(part, part, h_send.at[q, kind], h_recv.at[src], frame, to)

    def own_step(q):
        start, wide = PANELS[q]

        @pl.when(has_rows)
        def _():
            for j in range(start // 128, (start + wide) // 128):
                panel_step(own, own, own_hi, own_lo, 0, BLK, j)
            here = pl.ds(start % BLK, wide)
            held[start // BLK, cell, :, here] = own_hi[:, start:start + wide]
            for i in ORDER:
                panel_to(q, i, True).start()
                panel_to(q, i, False).start()

    def panel_forward(q, i, by_row):
        src, slot = (row_peer(i), i - 1) if by_row else (col_peer(i), i + 2)

        @pl.when(src >= PB)
        def _():
            part = block(q, src, 0, BLK)
            remote(part, part, l_send.at[q], l_recv.at[q, slot], frame, src).wait_recv()
            for k in ORDER:
                to = col_peer(k) if by_row else row_peer(k)

                @pl.when(to >= PB)
                def _(to=to):
                    half_to(q, 0 if by_row else 1, src, to).start()

    def forward_all(q):
        for i in ORDER:
            panel_forward(q, i, True)
            panel_forward(q, i, False)

    pivot_start()
    load_own.start()

    @pl.when(has_rows)
    def _():
        load_rest.start()

    pivot_send(0)
    pivot_send(1)
    load_own.wait()
    pivot_end(0)
    pivot_step(0)
    pivot_send(2)
    panel_step(raw, a, a_hi, a_lo, 128, 128, 0)
    pivot_step(1)
    own_step(0)
    pivot_end(1)
    for j in range(2):
        panel_step(raw, a, a_hi, a_lo, BLK, BLK, j)
    pivot_step(2)
    forward_all(0)
    panel_step(raw, a, a_hi, a_lo, 384, 128, 2)
    pivot_step(3)
    own_step(1)
    pivot_end(2)
    for j in range(4):
        panel_step(raw, a, a_hi, a_lo, 2 * BLK, BLK, j)
    pivot_step(4)
    forward_all(1)
    own_step(2)
    panel_step(raw, a, a_hi, a_lo, 640, 128, 4)
    pivot_step(5)
    own_step(3)
    forward_all(2)

    def order(t):
        pair, by_row = (t - 1) // 2, lax.rem(t - 1, 2) == 0
        i = jnp.where(pair == 0, 1, jnp.where(pair == 1, 3, 2))
        u = t - 7
        dy = jnp.where(t == 0, 0, jnp.where(t < 7, jnp.where(by_row, 0, i), 1 + u // 3))
        dz = jnp.where(t == 0, 0, jnp.where(t < 7, jnp.where(by_row, i, 0), 1 + lax.rem(u, 3)))
        return lax.rem(y + dy, SIDE) * SIDE + lax.rem(z + dz, SIDE)

    whole = pl.ds(0, BLK)

    def x_copy(kind, c):
        source, rows, to = [
            (frame, whole, right), (frame, whole, left), (frame, whole, sibling),
            (left, pl.ds(0, HALF), right), (left, whole, sibling),
            (right, pl.ds(HALF, HALF), left), (right, whole, sibling),
            (across, whole, sibling),
        ][kind]
        dst = pieces.at[source, c, rows]
        src = chunk.at[c, rows] if kind < 3 else dst
        at = (near.at[c], near.at[c], late.at[0], far_sem.at[c], late.at[1], far_sem.at[c], late.at[2], late.at[3])
        return remote(src, dst, x_send.at[kind], at[kind], to, cell)

    def arrived(sem, region):
        remote(region, region, x_send.at[0], sem, sibling, cell).wait_recv()

    def keep(c):
        return pltpu.make_async_copy(chunk.at[c], pieces.at[frame, c], keep_sem)

    def step(t, carry):
        c = order(t)
        for n, i in enumerate(ORDER):
            @pl.when(t == 1 + n)
            def _(i=i):
                panel_forward(3, i, True)
                panel_forward(3, i, False)

        @pl.when((t < STEPS) & (c >= PB) & has_rows)
        def _():
            @pl.when(t == 0)
            def _():
                load_rest.wait()

            @pl.when(t >= 7)
            def _():
                part = held.at[:, c]
                remote(part, part, h_send.at[0, 0], h_recv.at[c], frame, cell).wait_recv()

            value = rest[:, pl.ds(pl.multiple_of((c - PB) * BLK, BLK), BLK)]
            for q in range(PB):
                value = value - lax.dot_general(
                    own_hi[:, BLK * q:BLK * (q + 1)], held[q, c], NT, preferred_element_type=F32
                )
            chunk[c] = value.astype(BF16)
            keep(c).start()
            for kind in range(3):
                x_copy(kind, c).start()

        back = order(t - LAG)

        @pl.when((t >= LAG) & (t < STEPS + LAG) & has_rows & (back >= PB))
        def _():
            arrived(near.at[back], pieces.at[pl.ds(0, 2), back])
            x_copy(3, back).start()
            x_copy(4, back).start()
            x_copy(5, back).start()
            x_copy(6, back).start()

        far = order(t - LAG2)

        @pl.when((t >= LAG2) & has_rows & (far >= PB))
        def _():
            arrived(far_sem.at[far], pieces.at[across, far])
            x_copy(7, far).start()

        return carry

    lax.fori_loop(0, STEPS + LAG2, step, 0)

    for r in range(PB):
        @pl.when(cell == r)
        def _(r=r):
            row_no = lax.broadcasted_iota(jnp.int32, (BLK, WIDTH), 0) + BLK * r
            col_no = lax.broadcasted_iota(jnp.int32, (BLK, WIDTH), 1)
            lower[...] = jnp.where(row_no >= col_no, a[BLK * r:BLK * (r + 1), :], 0.0)

    @pl.when(has_rows)
    def _():
        lower[...] = own[...]

    for r in range(PB):
        pivot_sent(r)
    for q, (_, wide) in enumerate(PANELS):
        @pl.when(has_rows)
        def _(q=q, wide=wide):
            part = held.at[0, pl.ds(0, 6), :, pl.ds(0, wide)]
            remote(part, part, l_send.at[q], l_recv.at[q, 0], frame, cell).wait_send()

        for count, when in (
            (9, (y != 0) & (z == SIDE - 1)), (6, (y != 0) & (z != SIDE - 1)),
            (3, (y == 0) & (z != SIDE - 1)),
        ):
            @pl.when(when)
            def _(q=q, count=count, wide=wide):
                part = held.at[0, pl.ds(0, count), pl.ds(0, HALF), pl.ds(0, wide)]
                for kind in range(2):
                    remote(part, part, h_send.at[q, kind], h_recv.at[0], frame, cell).wait_send()

    @pl.when(has_rows)
    def _():
        every = pl.ds(PB, CELLS - PB)
        full = pieces.at[frame, every]
        for n in range(4):
            arrived(late.at[n], full)
        pltpu.make_async_copy(chunk.at[every], full, keep_sem).wait()
        for kind in range(8):
            region = pieces.at[frame, every, pl.ds(0, HALF)] if kind in (3, 5) else full
            remote(region, region, x_send.at[kind], late.at[0], sibling, cell).wait_send()


def fronts(front):
    rest = CELLS * BLK - WIDTH
    return pl.pallas_call(
        fronts_kernel,
        out_shape=(
            jax.ShapeDtypeStruct((BLK, WIDTH), F32),
            jax.ShapeDtypeStruct((FRAMES, CELLS, BLK, BLK), BF16),
        ),
        in_specs=[pl.BlockSpec(memory_space=pl.ANY)],
        out_specs=(pl.BlockSpec(memory_space=VMEM), pl.BlockSpec(memory_space=pl.ANY)),
        scratch_shapes=[
            VMEM((WIDTH, WIDTH), F32), VMEM((WIDTH, WIDTH), F32),
            VMEM((WIDTH, WIDTH), BF16), VMEM((WIDTH, WIDTH), BF16),
            VMEM((BLK, WIDTH), F32), VMEM((BLK, WIDTH), BF16), VMEM((BLK, WIDTH), BF16),
            VMEM((WIDTH // 128, 128, 128), BF16), VMEM((WIDTH // 128, 128, 128), BF16),
            VMEM((128, 256), F32), VMEM((128, 256), F32),
            VMEM((PB, CELLS, BLK, BLK), BF16), VMEM((BLK, rest), F32), VMEM((CELLS, BLK, BLK), BF16),
            DMA((2,)), DMA((1,)), DMA((2, PB)), DMA((2,)), DMA((PB, 2)), DMA((PB, 2)),
            DMA((PB, 2)), DMA((PB,)),
            DMA((len(PANELS),)), DMA((len(PANELS), 6)), DMA((len(PANELS), 2)), DMA((CELLS,)),
            DMA((8,)), DMA((CELLS,)), DMA((CELLS,)), DMA((4,)), DMA,
        ],
        compiler_params=pltpu.CompilerParams(
            collective_id=1, has_side_effects=True, vmem_limit_bytes=56 << 20
        ),
        name="fronts",
    )(front)


GROUP = 4
SPAN = GROUP * BLK
WHOLE = CELLS // GROUP


def extend_kernel(parent_of, block_map, parent, pieces, out, total, buffer, table, sems):
    q, g = pl.program_id(0), pl.program_id(1)
    frame, cell = lax.axis_index("frame"), lax.axis_index("cell")
    turn = lax.rem(q, 2)

    @pl.when((q == 0) & (g == 0))
    def _():
        count, touched = 0, [0, 0]
        for c in range(FRAMES):
            live = ((parent_of[c] == frame) & (cell >= PB)).astype(jnp.int32)
            half = block_map[c, jnp.maximum(cell - PB, 0)] // CELLS
            table[count] = c
            table[CELLS + count] = half
            count = count + live
            touched = [touched[0] + live * (1 - half), touched[1] + live * half]
        table[2 * CELLS] = count
        table[2 * CELLS + 1], table[2 * CELLS + 2] = touched

    count = table[2 * CELLS]

    def fetch(n, at):
        slot = lax.rem(at, 2)
        return pltpu.make_async_copy(
            pieces.at[table[n], pl.ds(at * GROUP, GROUP)], buffer.at[slot, n], sems.at[slot, n]
        )

    def each(act):
        for n in range(FRAMES):
            @pl.when(n < count)
            def _(n=n):
                act(n)

    @pl.when((q == 0) & (g == 0))
    def _():
        each(lambda n: fetch(n, q).start())

    @pl.when((q + 1 < WHOLE) & (g == 0))
    def _():
        each(lambda n: fetch(n, q + 1).start())

    for h in range(2):
        used = table[2 * CELLS + 1 + h] > 0

        @pl.when(used)
        def _(h=h):
            total[h] = parent[h].astype(F32)

        @pl.when(jnp.logical_not(used))
        def _(h=h):
            out[h] = parent[h]

    @pl.when(g == 0)
    def _():
        each(lambda n: fetch(n, q).wait())

    def add(n):
        c, half = table[n], table[CELLS + n]
        for i in range(GROUP):
            block = q * GROUP + i

            @pl.when((block >= PB) & (block_map[c, jnp.maximum(block - PB, 0)] // CELLS == g))
            def _(i=i):
                total[half, :, i * BLK:(i + 1) * BLK] += buffer[turn, n, i].astype(F32)

    each(add)
    for h in range(2):
        @pl.when(table[2 * CELLS + 1 + h] > 0)
        def _(h=h):
            out[h] = total[h].astype(BF16)


def extend(parent_of, block_map, parent, pieces):
    tile = pl.BlockSpec((2, BLK, SPAN), lambda q, g, *_: (0, 0, g * WHOLE + q))
    return pl.pallas_call(
        extend_kernel,
        out_shape=jax.ShapeDtypeStruct(parent.shape, BF16),
        grid_spec=pltpu.PrefetchScalarGridSpec(
            num_scalar_prefetch=2,
            grid=(WHOLE, 2),
            in_specs=[tile, pl.BlockSpec(memory_space=pl.ANY)],
            out_specs=tile,
            scratch_shapes=[
                VMEM((2, BLK, SPAN), F32), VMEM((2, FRAMES, GROUP, BLK, BLK), BF16),
                pltpu.SMEM((3 * CELLS,), jnp.int32), DMA((2, FRAMES)),
            ],
        ),
        compiler_params=pltpu.CompilerParams(vmem_limit_bytes=60 << 20),
        name="extend",
    )(parent_of, block_map, parent, pieces)


def per_device(front, parent_of, block_map, parent_in):
    lower, pieces = fronts(front[0])
    out = extend(parent_of, block_map, parent_in[0], pieces)
    return lower[None], out[None]


def solution(mesh):
    placed = (P("frame", "cell", None), P(), P(), P("frame", None, "cell", None))
    return jax.shard_map(
        per_device,
        mesh=mesh,
        in_specs=placed,
        out_specs=(P("frame", "cell", None), P("frame", None, "cell", None)),
        check_vma=False,
    )
```
